1024 devices in a mesh: dp: 512 (over y, x_hi, z, core), mp: 2 (over x_lo).
Axes of the slice: x: 4 (x_hi: 2, x_lo: 2; x = x_hi * 2 + x_lo), y: 8, z: 16, core: 2. Of those that a mesh axis runs over, the one named last changes fastest.
Arguments:
- image_emb: float32 [131072, 1152], P(('dp', 'mp')), may hold values from -0.1875 to 0.1875
- text_emb: float32 [131072, 1152], P(('dp', 'mp')), may hold values from -0.1875 to 0.1875
- video_ids: int32 [131072], P(('dp', 'mp')), may hold values from 0 to 32767, never falling along the last dimension, each value on 1 to 8 neighbouring positions
- log_scale: float32 [], replicated, may hold values from 4 to 5
- bias: float32 [], replicated, may hold values from -6 to -2
Outputs:
- loss: float32 [], replicated
- grad_image: float32 [131072, 1152], P(('dp', 'mp'))
- grad_text: float32 [131072, 1152], P(('dp', 'mp'))
- grad_log_scale: float32 [], replicated
- grad_bias: float32 [], replicated
The draws below stay inside these ranges and needn't reach their ends.
Inputs may be any that keep to these rules, and one draw needn't show every extreme that they name: video_ids never fall along the rows; each video covers 1 to 8 consecutive pairs, one exactly 8.
All inputs are finite; a program needn't handle non-finite values.
Results may differ from the reference program's by a relative error of at most 0.00015.
Values sent between devices are 32-bit elements; how exact they have to be, the bound alone decides.
No kernel may reach another device: no remote copies, remote signals or barrier semaphores. Data moves between devices by JAX's collectives and lax.ppermute only.
A program may use at most 32 MiB of HBM per device.

```python
import math
import jax
import jax.numpy as jnp
import numpy as np
from jax import lax

D = 1152
ROWS = 128
STEPS = 7
TOKENS = 131072


def block_scale(own_key, shape, pieces, smallest, top_value):
    def one(axis_at, blocks):
        draws = jax.random.uniform(jax.random.fold_in(jax.random.fold_in(own_key, 6), axis_at), (blocks,), jnp.float32, smallest / len(pieces), top_value / len(pieces))
        return jnp.repeat(jnp.exp(draws), shape[axis_at] // blocks).reshape((-1,) + (1,) * (len(shape) - axis_at - 1))

    gain = one(*pieces[0])
    for cut in pieces[1:]:
        gain = gain * one(*cut)
    return gain


def length_profile(amount, total, reach, skew):
    portions = [(1 << 20) // math.isqrt(grade ** skew) + 1 for grade in range(2, amount + 1)]
    surplus, counts = total - reach - (amount - 1), [1] * (amount - 1)
    while surplus > 0:
        movable = [i for i in range(amount - 1) if counts[i] < reach]
        pool, budget = sum([portions[i] for i in movable]), surplus
        for i in movable:
            extra = min(reach - counts[i], max(1, budget * portions[i] // pool), surplus)
            counts[i] = counts[i] + extra
            surplus = surplus - extra
    return np.array([reach] + counts)


def ragged_sizes(key, count, total, bound, skew):
    if count == 2:
        one = jax.random.randint(key, (), max(1, total - bound), min(bound, total - 1) + 1)
        return jnp.stack([one, total - one])
    lengths = jnp.asarray(length_profile(count, total, bound, skew), jnp.int32)
    twos = (count - 1) // 2
    giver, receiver = lengths[1:1 + 2 * twos:2], lengths[2:2 + 2 * twos:2]
    margin = jnp.minimum(giver - 1, bound - receiver)
    moved = jax.random.randint(jax.random.fold_in(key, 1), (twos,), 0, 1 << 20) % (margin + 1)
    lengths = lengths.at[1:1 + 2 * twos:2].set(giver - moved).at[2:2 + 2 * twos:2].set(receiver + moved)
    return lengths[jax.random.permutation(jax.random.fold_in(key, 2), count)]


def centred(own_key, dims, scale, limit, pieces=(), kind=jnp.bfloat16):
    result = scale * jax.random.normal(own_key, dims, jnp.float32)
    if pieces:
        result = result * block_scale(own_key, dims, pieces, -0.22, 0.18)
    return jnp.clip(result, -limit, limit).astype(kind)


def setup_inputs(seed: int = 0) -> dict:
    streams_of = jax.random.split(jax.random.key(seed), 6)
    image_emb = centred(streams_of[0], (TOKENS, D), D ** -0.5, 0.1875, ((0, 1024),), jnp.float32)
    text_emb = centred(streams_of[1], (TOKENS, D), D ** -0.5, 0.1875, ((0, 1024),), jnp.float32)
    video_ids = jnp.searchsorted(jnp.cumsum(ragged_sizes(streams_of[2], TOKENS // 4, TOKENS, 8, 0)), jnp.arange(TOKENS), side="right").astype(jnp.int32)
    log_scale = jnp.clip(jax.random.uniform(streams_of[3], (), jnp.float32, 4.0, 5.0), 4.0, 5.0)
    bias = jnp.clip(jax.random.uniform(streams_of[4], (), jnp.float32, -6.0, -2.0), -6.0, -2.0)
    return dict(image_emb=image_emb, text_emb=text_emb, video_ids=video_ids, log_scale=log_scale, bias=bias)


def reference(image_emb, text_emb, video_ids, log_scale, bias):
    scale = jnp.exp(log_scale)
    norm = 1.0 / (STEPS * ROWS)
    blocks = TOKENS // ROWS
    images = image_emb.reshape(blocks, ROWS, D)
    texts = text_emb.reshape(blocks, ROWS, D)
    ids = video_ids.reshape(blocks, ROWS)
    image_grad = jnp.zeros_like(images)
    text_grad = jnp.zeros_like(texts)
    loss_sum = jnp.zeros((), jnp.float32)
    scale_sum = jnp.zeros((), jnp.float32)
    bias_sum = jnp.zeros((), jnp.float32)
    for step in range(STEPS):
        rolled = jnp.roll(texts, step, axis=0)
        other = jnp.roll(ids, step, axis=0)
        sim = jnp.einsum("nrd,ncd->nrc", images, rolled, precision=lax.Precision.HIGHEST)
        sign = jnp.where(ids[:, :, None] == other[:, None, :], 1.0, -1.0).astype(sim.dtype)
        shifted = sign * (scale * sim + bias)
        loss_sum = loss_sum + norm * jnp.sum(jax.nn.softplus(-shifted))
        weight = -sign * jax.nn.sigmoid(-shifted) * norm
        image_grad = image_grad + scale * jnp.einsum("nrc,ncd->nrd", weight, rolled, precision=lax.Precision.HIGHEST)
        part = scale * jnp.einsum("nrc,nrd->ncd", weight, images, precision=lax.Precision.HIGHEST)
        text_grad = text_grad + jnp.roll(part, -step, axis=0)
        scale_sum = scale_sum + scale * jnp.sum(weight * sim)
        bias_sum = bias_sum + jnp.sum(weight)
    return (loss_sum / TOKENS, image_grad.reshape(TOKENS, D), text_grad.reshape(TOKENS, D), scale_sum / TOKENS, bias_sum / TOKENS)
```

```python
import functools

import jax
import jax.numpy as jnp
from jax import lax
from jax.experimental import pallas as pl
from jax.experimental.pallas import tpu as pltpu
from jax.sharding import Mesh
from jax.sharding import PartitionSpec as P

STEPS = 7
LINES, DEEP = 16, 16
SHAPE = (2, 4, 2, 4, 4, 2, 2)
NAMES = ("y_hi", "y_lo", "x_hi", "z_hi", "z_lo", "core", "x_lo")
F32, BF16 = jnp.float32, jnp.bfloat16
VMEM = pl.BlockSpec(memory_space=pltpu.VMEM)
SMEM = pl.BlockSpec(memory_space=pltpu.SMEM)


def up(b):
    plane, pos = divmod(b, 4)
    if plane % DEEP < DEEP - 1:
        return b + 4
    return (plane + 1) % (LINES * DEEP) * 4 + (pos ^ 1)


def down(b):
    plane, pos = divmod(b, 4)
    if plane % DEEP > 0:
        return b - 4
    return (plane - 1) % (LINES * DEEP) * 4 + (pos ^ 1)


def halves(x):
    high = x.astype(BF16)
    return high, (x - high.astype(F32)).astype(BF16)


def product(a, b, dims):
    dot = functools.partial(lax.dot_general, dimension_numbers=(dims, ((), ())), preferred_element_type=F32)
    return dot(a[0], b[0]) + (dot(a[0], b[1]) + dot(a[1], b[0]))


def column(row):
    return jnp.transpose(jnp.broadcast_to(row, (row.shape[1], row.shape[1])))


def band(rows, cols, dists, own, beside, log_scale, bias):
    size, width = rows[0].shape
    left = halves(jnp.concatenate([row[...] for row in rows], 0))
    right = halves(jnp.concatenate([col[...] for col in cols], 0))
    sim = product(left, right, ((1,), (1,)))
    scale = jnp.exp(jnp.full((1, size), log_scale, F32))
    norm = 1.0 / (STEPS * size)
    loss = slope = plain = jnp.zeros((size, size), F32)
    weights = []
    for a in range(len(rows)):
        line = []
        mine = None if own[a] is None else column(own[a])
        for b in range(len(cols)):
            part = sim[a * size : (a + 1) * size, b * size : (b + 1) * size]
            dist, counts = dists[a][b]
            keep = jnp.where((dist >= 0) & (dist < STEPS) & counts, norm, 0.0).astype(F32)
            if mine is None:
                sign = -1.0
            else:
                other = jnp.where(dist == 0, own[a], jnp.where(dist == 1, beside[a], -1.0))
                sign = jnp.where(mine == other, 1.0, -1.0)
            u = sign * (scale * part + bias)
            small = jnp.exp(-jnp.abs(u))
            weight = -sign * (jnp.where(u >= 0, small, 1.0) / (1.0 + small)) * keep
            loss = loss + (jnp.maximum(-u, 0.0) + jnp.log1p(small)) * keep
            slope = slope + weight * part
            plain = plain + weight
            line.append(weight)
        weights.append(jnp.concatenate(line, 1))
    grads = product(halves(jnp.concatenate(weights, 0)), right, ((1,), (0,)))
    return jnp.exp(jnp.full((1, width), log_scale, F32)) * grads, (loss, scale * slope, plain)


def totals(sums):
    lane = lax.broadcasted_iota(jnp.int32, (1, 128), 1)
    loss, slope, plain = (jnp.sum(part) for part in sums)
    return jnp.where(lane == 0, loss, jnp.where(lane == 1, slope, jnp.where(lane == 2, plain, 0.0)))


def tags(ids):
    own = ids[0:1, :], ids[8:9, :], None
    before = ids[1:2, :], ids[9:10, :], None
    after = ids[2:3, :], ids[10:11, :], None
    return own, before, after


def plane_kernel(place, params, ids, i0, i1, i2, t0, t1, t2, images, texts, sums):
    own, before, after = tags(ids)
    p = place[0]
    rows, cols = (p, p ^ 2), (p, p ^ 1)
    dists = [[(i - t, True) for t in cols] for i in rows]
    images[...], parts = band((i0, i2), (t0, t1), dists, own, before, params[0], params[1])
    sums[...] = totals(parts)
    dists = [[(i - t, True) for i in cols] for t in rows]
    texts[...], _ = band((t0, t2), (i0, i1), dists, own, after, params[0], params[1])


def lower_kernel(place, params, ids, i0, i2, cross, u0, u1, images_in, sums_in, images, sums):
    own, before, _ = tags(ids)
    p, q, r, core = place[0], place[1], place[2], place[3]
    dists = [[(i + 4 - t, True) for t in (q, q ^ 1)] for i in (p, p ^ 2)]
    dists.append([((r ^ 2) + 8 - t, core == 1) for t in (q, q ^ 1)])
    grads, parts = band((i0, i2, cross), (u0, u1), dists, own, before, params[0], params[1])
    both = images_in.shape[0]
    images[0:both, :] = images_in[...] + grads[0:both, :]
    images[both:, :] = grads[both:, :]
    sums[...] = sums_in[...] + totals(parts)


def upper_kernel(place, params, ids, t0, t2, cross, d0, d1, texts_in, images_in, texts, swap, far):
    own, _, after = tags(ids)
    p, q, r, core = place[0], place[1], place[2], place[3]
    dists = [[(i + 4 - t, True) for i in (r, r ^ 1)] for t in (p, p ^ 2)]
    dists.append([(i + 8 - (q ^ 2), core == 0) for i in (r, r ^ 1)])
    grads, _ = band((t0, t2, cross), (d0, d1), dists, own, after, params[0], params[1])
    size = texts.shape[0]
    texts[...] = texts_in[0:size, :] + grads[0:size, :]
    swap[0:size, :] = images_in[size : 2 * size, :]
    swap[size:, :] = texts_in[size:, :] + grads[size : 2 * size, :]
    far[...] = jnp.where(core == 1, images_in[2 * size :, :], grads[2 * size :, :])


def kernel_call(body, name, shapes, rows, cols, passes):
    size, width = 128, 1152
    cost = pl.CostEstimate(
        flops=12 * passes * rows * cols * width,
        bytes_accessed=4 * width * (rows + cols) * 2,
        transcendentals=2 * rows * cols,
    )
    return lambda place, params, *blocks: pl.pallas_call(
        body,
        out_shape=[jax.ShapeDtypeStruct(shape, F32) for shape in shapes],
        in_specs=[SMEM, SMEM] + [VMEM] * len(blocks),
        out_specs=[VMEM] * len(shapes),
        compiler_params=pltpu.CompilerParams(vmem_limit_bytes=48 << 20),
        cost_estimate=cost,
        name=name,
    )(place, params, *blocks)


def local(image, text, video_ids, log_scale, bias):
    size, width = image.shape
    count = lax.axis_size(NAMES)
    everyone = range(count)

    def send(x, to):
        return lax.ppermute(x, NAMES, [(b, to(b)) for b in everyone])

    def other_core(x):
        return send(x, lambda b: b ^ 2)

    plane_z = lax.axis_index(("z_hi", "z_lo"))
    core = lax.axis_index("core")
    p = 2 * core + lax.axis_index("x_lo")
    q = jnp.where(plane_z > 0, p, p ^ 1)
    r = jnp.where(plane_z < DEEP - 1, p, p ^ 1)
    place = jnp.stack([p, q, r, core]).astype(jnp.int32)
    params = jnp.stack([log_scale, bias])

    t0, i0 = text, image
    u0 = send(t0, up)
    t1 = send(t0, lambda b: b ^ 1)
    d0 = send(i0, down)
    i1 = send(i0, lambda b: b ^ 1)
    t2, i2 = other_core(t0), other_core(i0)
    u1 = send(t1, up)
    d1 = send(i1, down)
    cross = other_core(jnp.where(core == 1, u0, d0))

    ids = video_ids.astype(F32)[None]
    before = send(ids, lambda b: (b + 1) % count)
    after = send(ids, lambda b: (b - 1) % count)
    mine = jnp.concatenate([ids, before, after, jnp.zeros((5, size), F32)], 0)
    ids = jnp.concatenate([mine, other_core(mine)], 0)

    wide = lambda n: (n * size, width)
    images, texts, sums = kernel_call(plane_kernel, "plane", (wide(2), wide(2), (1, 128)), 256, 256, 2)(
        place, params, ids, i0, i1, i2, t0, t1, t2
    )
    images, sums = kernel_call(lower_kernel, "lower", (wide(3), (1, 128)), 384, 256, 1)(
        place, params, ids, i0, i2, cross, u0, u1, images, sums
    )
    sums = lax.psum(lax.psum(sums, "core"), ("x_hi", "x_lo"))
    d1, sums = lax.optimization_barrier((d1, sums))
    texts, swap, far = kernel_call(upper_kernel, "upper", (wide(1), wide(2), wide(1)), 384, 256, 1)(
        place, params, ids, t0, t2, cross, d0, d1, texts, images
    )
    swap = other_core(swap)
    far = send(far, lambda b: (down(b) if b % 4 < 2 else up(b)) ^ 2)
    sums = lax.psum(lax.psum(lax.psum(sums, "z_lo"), "z_hi"), ("y_hi", "y_lo"))
    grad_image = images[:size] + swap[:size] + jnp.where(core == 0, far, 0.0)
    grad_text = texts + swap[size:] + jnp.where(core == 1, far, 0.0)
    tokens = size * count
    return sums[0, 0] / tokens, grad_image, grad_text, sums[0, 1] / tokens, sums[0, 2] / tokens


def solution(mesh):
    fine = Mesh(mesh.devices.reshape(SHAPE), NAMES)
    rows = P(NAMES, None)
    return jax.shard_map(
        local,
        mesh=fine,
        in_specs=(rows, rows, P(NAMES), P(), P()),
        out_specs=(P(), rows, rows, P(), P()),
        check_vma=False,
    )
```

```python
import functools

import jax
import jax.numpy as jnp
from jax import lax
from jax.experimental import pallas as pl
from jax.experimental.pallas import tpu as pltpu
from jax.sharding import Mesh
from jax.sharding import PartitionSpec as P

STEPS = 7
LINES, DEEP = 16, 16
SHAPE = (2, 4, 2, 4, 4, 2, 2)
NAMES = ("y_hi", "y_lo", "x_hi", "z_hi", "z_lo", "core", "x_lo")
F32, BF16 = jnp.float32, jnp.bfloat16
VMEM = pl.BlockSpec(memory_space=pltpu.VMEM)
SMEM = pl.BlockSpec(memory_space=pltpu.SMEM)


def up(b):
    plane, pos = divmod(b, 4)
    if plane % DEEP < DEEP - 1:
        return b + 4
    return (plane + 1) % (LINES * DEEP) * 4 + (pos ^ 1)


def down(b):
    plane, pos = divmod(b, 4)
    if plane % DEEP > 0:
        return b - 4
    return (plane - 1) % (LINES * DEEP) * 4 + (pos ^ 1)


def halves(x):
    high = x.astype(BF16)
    return high, (x - high.astype(F32)).astype(BF16)


def joined(*pairs):
    return tuple(jnp.concatenate(parts, 0) for parts in zip(*pairs))


def product(a, b, dims):
    dot = functools.partial(lax.dot_general, dimension_numbers=(dims, ((), ())), preferred_element_type=F32)
    return dot(a[0], b[0]) + (dot(a[0], b[1]) + dot(a[1], b[0]))


def gradient(weights, cols, log_scale):
    grads = product(halves(weights), cols, ((1,), (0,)))
    return jnp.exp(jnp.full((1, grads.shape[1]), log_scale, F32)) * grads


def column(row):
    return jnp.transpose(jnp.broadcast_to(row, (row.shape[1], row.shape[1])))


def weigh(sim, dists, own, before, log_scale, bias, tokens):
    size = 128
    scale = jnp.exp(jnp.full((1, size), log_scale, F32))
    norm = 1.0 / (STEPS * size)
    loss = slope = plain = jnp.zeros((size, size), F32)
    weights = []
    for a, row in enumerate(dists):
        line = []
        mine = None if own[a] is None else column(own[a])
        for b, (dist, counts) in enumerate(row):
            part = sim[a * size : (a + 1) * size, b * size : (b + 1) * size]
            keep = jnp.where((dist >= 0) & (dist < STEPS) & counts, norm, 0.0).astype(F32)
            if mine is None:
                sign = -1.0
            else:
                other = jnp.where(dist == 0, own[a], jnp.where(dist == 1, before[a], -1.0))
                sign = jnp.where(mine == other, 1.0, -1.0)
            u = sign * (scale * part + bias)
            small = jnp.exp(-jnp.abs(u))
            weight = -sign * (jnp.where(u >= 0, small, 1.0) / (1.0 + small)) * keep
            loss = loss + (jnp.maximum(-u, 0.0) + jnp.log1p(small)) * keep
            slope = slope + weight * part
            plain = plain + weight
            line.append(weight)
        weights.append(jnp.concatenate(line, 1))
    lane = lax.broadcasted_iota(jnp.int32, (1, size), 1)
    loss, slope, plain = jnp.sum(loss), jnp.sum(scale * slope), jnp.sum(plain)
    sums = jnp.where(lane == 0, loss, jnp.where(lane == 1, slope, jnp.where(lane == 2, plain, 0.0)))
    return jnp.concatenate(weights, 0), sums * (1.0 / tokens)


def tags(ids):
    return (ids[0:1, :], ids[8:9, :], None), (ids[1:2, :], ids[9:10, :], None)


def ready_kernel(image, text, i_high, i_low, t_high, t_low):
    i_high[...], i_low[...] = halves(image[...])
    t_high[...], t_low[...] = halves(text[...])


def first_kernel(
    tokens, place, params, ids, i_high, i_low, i2, far, t_high, t_low, t1, u0, high, low, images, gt0, gt1, gu0, sums
):
    own, before = tags(ids)
    p, q, r, core = place[0], place[1], place[2], place[3]
    size = t1.shape[0]
    rows = joined((i_high[...], i_low[...]), halves(i2[...]), halves(far[...]))
    high[...], low[...] = rows
    cols = joined((t_high[...], t_low[...]), halves(t1[...]), halves(u0[...]))
    dists = [[(i - p, True), (i - (p ^ 1), True), (i + 4 - q, True)] for i in (p, p ^ 2)]
    dists.append([(0, False), (0, False), ((r ^ 2) + 8 - q, core == 1)])
    sim = product(rows, cols, ((1,), (1,)))
    weights, sums[...] = weigh(sim, dists, own, before, params[0], params[1], tokens)
    images[...] = gradient(weights, cols, params[0])
    texts = gradient(jnp.transpose(weights), rows, params[0])
    gt0[...] = texts[0:size, :]
    gt1[...] = texts[size : 2 * size, :]
    gu0[...] = texts[2 * size :, :]


def last_kernel(tokens, place, params, ids, high, low, u1, images, sums_in, gi0, gi2, gfar, gu1, sums):
    own, before = tags(ids)
    p, q, r, core = place[0], place[1], place[2], place[3]
    size = u1.shape[0]
    rows, cols = (high[...], low[...]), halves(u1[...])
    dists = [[(i + 4 - (q ^ 1), True)] for i in (p, p ^ 2)]
    dists.append([((r ^ 2) + 8 - (q ^ 1), core == 1)])
    sim = product(rows, cols, ((1,), (1,)))
    weights, parts = weigh(sim, dists, own, before, params[0], params[1], tokens)
    sums[...] = sums_in[...] + parts
    grads = images[...] + gradient(weights, cols, params[0])
    gi0[...] = grads[0:size, :]
    gi2[...] = grads[size : 2 * size, :]
    gfar[...] = grads[2 * size :, :]
    gu1[...] = gradient(jnp.transpose(weights), rows, params[0])


def kernel_call(body, name, shapes, rows, cols, *args, scalars=2):
    cost = pl.CostEstimate(
        flops=18 * rows * cols * 1152, bytes_accessed=8 * 1152 * (rows + cols), transcendentals=2 * rows * cols
    )
    return pl.pallas_call(
        body,
        out_shape=[jax.ShapeDtypeStruct(shape, dtype) for shape, dtype in shapes],
        in_specs=[SMEM] * scalars + [VMEM] * (len(args) - scalars),
        out_specs=[VMEM] * len(shapes),
        compiler_params=pltpu.CompilerParams(vmem_limit_bytes=16 << 20),
        cost_estimate=cost,
        name=name,
    )(*args)


def local(image, text, video_ids, log_scale, bias):
    size, width = image.shape
    count = lax.axis_size(NAMES)
    tokens = size * count
    everyone = range(count)

    def send(x, to, senders=everyone):
        return lax.ppermute(x, NAMES, [(b, to(b)) for b in senders])

    def other_core(x):
        return send(x, lambda b: b ^ 2)

    def beside(x):
        return send(x, lambda b: b ^ 1)

    plane_z = lax.axis_index(("z_hi", "z_lo"))
    core = lax.axis_index("core")
    p = 2 * core + lax.axis_index("x_lo")
    q = jnp.where(plane_z > 0, p, p ^ 1)
    r = jnp.where(plane_z < DEEP - 1, p, p ^ 1)
    place = jnp.stack([p, q, r, core]).astype(jnp.int32)
    params = jnp.stack([log_scale, bias])

    t1 = beside(text)
    ids = video_ids.astype(F32)[None]
    before = send(ids, lambda b: (b + 1) % count)
    near_text, near_image, before = lax.optimization_barrier((text, image, before))
    u0 = send(near_text, up)
    mine = jnp.concatenate([ids, before, jnp.zeros((6, size), F32)], 0)
    ids = jnp.concatenate([mine, other_core(mine)], 0)
    i2 = other_core(near_image)
    far = send(near_image, lambda b: down(b) ^ 2, [b for b in everyone if b % 4 < 2])
    half = ((size, width), BF16)
    ready = kernel_call(ready_kernel, "ready", [half] * 4, 2, 2, image, text, scalars=0)
    u0, t1, i_high, i_low, t_high, t_low = lax.optimization_barrier((u0, t1, *ready))
    u1 = send(t1, up)

    block, three, row = ((size, width), F32), (3 * size, width), ((1, size), F32)
    high, low, images, gt0, gt1, gu0, sums = kernel_call(
        functools.partial(first_kernel, tokens),
        "first",
        [(three, BF16), (three, BF16), (three, F32), block, block, block, row],
        384,
        384,
        *(place, params, ids, i_high, i_low, i2, far, t_high, t_low, t1, u0),
    )
    gt1, gu0 = beside(gt1), send(gu0, down)
    gi0, gi2, gfar, gu1, sums = kernel_call(
        functools.partial(last_kernel, tokens),
        "last",
        [block, block, block, block, row],
        384,
        128,
        *(place, params, ids, high, low, u1, images, sums),
    )
    gu1 = send(gu1, lambda b: down(b) ^ 1)
    gi2 = other_core(gi2)
    gfar = send(gfar, lambda b: up(b) ^ 2, [b for b in everyone if b % 4 >= 2])
    sums, gt1, gu0 = lax.optimization_barrier((sums, gt1, gu0))

    def add_up(row, axes):
        shares = jnp.broadcast_to(row, (lax.axis_size(axes), size))
        return jnp.sum(lax.all_to_all(shares, axes, 0, 0, tiled=True), axis=0, keepdims=True)

    sums = add_up(sums, ("z_hi", "z_lo"))
    sums, gu1, gi2, gfar = lax.optimization_barrier((sums, gu1, gi2, gfar))
    sums = add_up(sums, ("y_hi", "y_lo", "x_hi", "core", "x_lo"))
    grad_image = gi0 + gi2 + gfar
    grad_text = gt0 + gt1 + gu0 + gu1
    return sums[0, 0], grad_image, grad_text, sums[0, 1], sums[0, 2]


def solution(mesh):
    fine = Mesh(mesh.devices.reshape(SHAPE), NAMES)
    rows = P(NAMES, None)
    return jax.shard_map(
        local,
        mesh=fine,
        in_specs=(rows, rows, P(NAMES), P(), P()),
        out_specs=(P(), rows, rows, P(), P()),
        check_vma=False,
    )
```

```python
import functools

import jax
import jax.numpy as jnp
from jax import lax
from jax.experimental import pallas as pl
from jax.experimental.pallas import tpu as pltpu
from jax.sharding import Mesh
from jax.sharding import PartitionSpec as P

STEPS = 7
LINES, DEEP = 16, 16
SHAPE = (2, 4, 2, 4, 4, 2, 2)
NAMES = ("y_hi", "y_lo", "x_hi", "z_hi", "z_lo", "core", "x_lo")
F32, BF16 = jnp.float32, jnp.bfloat16
VMEM = pl.BlockSpec(memory_space=pltpu.VMEM)
SMEM = pl.BlockSpec(memory_space=pltpu.SMEM)


def up(b):
    plane, pos = divmod(b, 4)
    if plane % DEEP < DEEP - 1:
        return b + 4
    return (plane + 1) % (LINES * DEEP) * 4 + (pos ^ 1)


def down(b):
    plane, pos = divmod(b, 4)
    if plane % DEEP > 0:
        return b - 4
    return (plane - 1) % (LINES * DEEP) * 4 + (pos ^ 1)


def halves(x):
    high = x.astype(BF16)
    return high, (x - high.astype(F32)).astype(BF16)


def joined(*pairs):
    return tuple(jnp.concatenate(parts, 0) for parts in zip(*pairs))


def product(a, b, dims):
    dot = functools.partial(lax.dot_general, dimension_numbers=(dims, ((), ())), preferred_element_type=F32)
    return dot(a[0], b[0]) + (dot(a[0], b[1]) + dot(a[1], b[0]))


def long_product(a, b, dims):
    left = jnp.concatenate([a[0], a[0], a[1]], dims[0][0])
    right = jnp.concatenate([b[0], b[1], b[0]], dims[1][0])
    return lax.dot_general(left, right, (dims, ((), ())), preferred_element_type=F32)


def gradient(weights, cols, log_scale, product):
    grads = product(halves(weights), cols, ((1,), (0,)))
    return jnp.exp(jnp.full((1, grads.shape[1]), log_scale, F32)) * grads


def tag(packet):
    return packet[128:129, 0:128]


def column(row):
    return jnp.transpose(jnp.broadcast_to(row, (row.shape[1], row.shape[1])))


def weigh(sim, dists, row_ids, col_ids, log_scale, bias, tokens):
    size = 128
    scale = jnp.exp(jnp.full((1, size), log_scale, F32))
    norm = 1.0 / (STEPS * size)
    loss = slope = plain = jnp.zeros((size, size), F32)
    weights = []
    for a, row in enumerate(dists):
        line = []
        mine = column(row_ids[a]) if a < len(row_ids) else None
        for b, (dist, counts) in enumerate(row):
            part = sim[a * size : (a + 1) * size, b * size : (b + 1) * size]
            keep = jnp.where((dist >= 0) & (dist < STEPS) & counts, norm, 0.0).astype(F32)
            if mine is None:
                sign = -1.0
            else:
                other = jnp.where((dist == 0) | (dist == 1), col_ids[b], -1.0)
                sign = jnp.where(mine == other, 1.0, -1.0)
            u = sign * (scale * part + bias)
            small = jnp.exp(-jnp.abs(u))
            weight = -sign * (jnp.where(u >= 0, small, 1.0) / (1.0 + small)) * keep
            loss = loss + (jnp.maximum(-u, 0.0) + jnp.log1p(small)) * keep
            slope = slope + weight * part
            plain = plain + weight
            line.append(weight)
        weights.append(jnp.concatenate(line, 1))
    lane = lax.broadcasted_iota(jnp.int32, (1, size), 1)
    loss, slope, plain = jnp.sum(loss), jnp.sum(scale * slope), jnp.sum(plain)
    sums = jnp.where(lane == 0, loss, jnp.where(lane == 1, slope, jnp.where(lane == 2, plain, 0.0)))
    return jnp.concatenate(weights, 0), sums * (1.0 / tokens)


def first_kernel(
    tokens, place, params, own, i2, far, t1, u0, image, text,
    high, low, images, gt0, gt1, gu0, mate, sums, i0, t0, arrived,
):
    copies = [
        pltpu.make_async_copy(source, target, arrived.at[n])
        for n, (source, target) in enumerate(((image, i0), (text, t0)))
    ]
    for copy in copies:
        copy.start()
    p, q, r, core = place[0], place[1], place[2], place[3]
    size = image.shape[0]
    both = 2 * size
    lone_rows, lone_cols = halves(far[...]), halves(u0[0:size, :])
    sim = product(lone_rows, lone_cols, ((1,), (1,)))
    lone, parts = weigh(sim, [[((r ^ 2) + 8 - q, core == 1)]], (), (), params[0], params[1], tokens)
    images[both:, :] = gradient(lone, lone_cols, params[0], product)
    gu0[...] = gradient(jnp.transpose(lone), lone_rows, params[0], product)
    high[both:, :], low[both:, :] = lone_rows
    mate_rows, near_cols = halves(i2[0:size, :]), halves(t1[0:size, :])
    for copy in copies:
        copy.wait()
    rows = joined(halves(i0[...]), mate_rows)
    high[0:both, :], low[0:both, :] = rows
    cols = joined(halves(t0[...]), near_cols, lone_cols)
    dists = [[(i - p, True), (i - (p ^ 1), True), (i + 4 - q, True)] for i in (p, p ^ 2)]
    sim = long_product(rows, cols, ((1,), (1,)))
    mate[...] = tag(i2)
    row_ids, col_ids = (own[...], mate[...]), (own[...], tag(t1), tag(u0))
    weights, more = weigh(sim, dists, row_ids, col_ids, params[0], params[1], tokens)
    sums[...] = parts + more
    images[0:both, :] = gradient(weights, cols, params[0], long_product)
    texts = gradient(jnp.transpose(weights), rows, params[0], long_product)
    gt0[...] = texts[0:size, :]
    gt1[...] = texts[size:both, :]
    gu0[...] += texts[both:, :]


def last_kernel(tokens, place, params, own, mate, high, low, u1, images, sums_in, gi0, gi2, gfar, gu1, sums):
    p, q, r, core = place[0], place[1], place[2], place[3]
    size = own.shape[1]
    rows, cols = (high[...], low[...]), halves(u1[0:size, :])
    dists = [[(i + 4 - (q ^ 1), True)] for i in (p, p ^ 2)]
    dists.append([((r ^ 2) + 8 - (q ^ 1), core == 1)])
    sim = product(rows, cols, ((1,), (1,)))
    weights, parts = weigh(sim, dists, (own[...], mate[...]), (tag(u1),), params[0], params[1], tokens)
    sums[...] = sums_in[...] + parts
    grads = images[...] + gradient(weights, cols, params[0], product)
    gi0[...] = grads[0:size, :]
    gi2[...] = grads[size : 2 * size, :]
    gfar[...] = grads[2 * size :, :]
    gu1[...] = gradient(jnp.transpose(weights), rows, params[0], product)


def kernel_call(body, name, shapes, rows, cols, *args, plain=0):
    cost = pl.CostEstimate(
        flops=18 * rows * cols * 1152, bytes_accessed=8 * 1152 * (rows + cols), transcendentals=2 * rows * cols
    )
    near = len(args) - plain
    far = [pltpu.with_memory_space_constraint(arg, pltpu.HBM) for arg in args[near:]]
    block = pltpu.VMEM((128, 1152), F32)
    return pl.pallas_call(
        body,
        out_shape=[jax.ShapeDtypeStruct(shape, dtype) for shape, dtype in shapes],
        in_specs=[SMEM, SMEM] + [VMEM] * (near - 2) + [pl.BlockSpec(memory_space=pltpu.HBM)] * plain,
        out_specs=[VMEM] * len(shapes),
        scratch_shapes=[block] * plain + [pltpu.SemaphoreType.DMA((plain,))] * (plain > 0),
        compiler_params=pltpu.CompilerParams(vmem_limit_bytes=16 << 20),
        cost_estimate=cost,
        name=name,
    )(*args[:near], *far)


def local(image, text, video_ids, log_scale, bias):
    size, width = image.shape
    count = lax.axis_size(NAMES)
    tokens = size * count
    everyone = range(count)

    def send(x, to, senders=everyone):
        return lax.ppermute(x, NAMES, [(b, to(b)) for b in senders])

    def other_core(x):
        return send(x, lambda b: b ^ 2)

    def beside(x):
        return send(x, lambda b: b ^ 1)

    plane_z = lax.axis_index(("z_hi", "z_lo"))
    core = lax.axis_index("core")
    p = 2 * core + lax.axis_index("x_lo")
    q = jnp.where(plane_z > 0, p, p ^ 1)
    r = jnp.where(plane_z < DEEP - 1, p, p ^ 1)
    place = jnp.stack([p, q, r, core]).astype(jnp.int32)
    params = jnp.stack([log_scale, bias])

    own = video_ids.astype(F32)[None]
    label = jnp.pad(own, ((0, 7), (0, width - size)))
    packet = jnp.concatenate([text, label], 0)
    t1 = beside(packet)
    u0 = send(packet, up)
    far = send(image, lambda b: down(b) ^ 2, [b for b in everyone if b % 4 < 2])
    label = lax.optimization_barrier(label)
    i2 = other_core(jnp.concatenate([image, label], 0))
    t1, place, params = lax.optimization_barrier((t1, place, params))
    u1 = send(t1, up)

    block, three, row = ((size, width), F32), (3 * size, width), ((1, size), F32)
    high, low, images, gt0, gt1, gu0, mate, sums = kernel_call(
        functools.partial(first_kernel, tokens),
        "first",
        [(three, BF16), (three, BF16), (three, F32), block, block, block, row, row],
        384,
        384,
        *(place, params, own, i2, far, t1, u0, image, text),
        plain=2,
    )
    gt1, gu0 = beside(gt1), send(gu0, down)
    gi0, gi2, gfar, gu1, sums = kernel_call(
        functools.partial(last_kernel, tokens),
        "last",
        [block, block, block, block, row],
        384,
        128,
        *(place, params, own, mate, high, low, u1, images, sums),
    )
    gu1 = send(gu1, lambda b: down(b) ^ 1)
    gi2 = other_core(gi2)
    gfar = send(gfar, lambda b: up(b) ^ 2, [b for b in everyone if b % 4 >= 2])

    def add_up(row, axes):
        shares = jnp.broadcast_to(row, (lax.axis_size(axes), size))
        return jnp.sum(lax.all_to_all(shares, axes, 0, 0, tiled=True), axis=0, keepdims=True)

    sums = add_up(sums, ("y_hi", "y_lo"))
    sums = add_up(sums, ("x_hi", "core", "x_lo"))
    sums, gt1, gu0, gu1, gi2, gfar = lax.optimization_barrier((sums, gt1, gu0, gu1, gi2, gfar))
    sums = add_up(sums, ("z_hi", "z_lo"))
    grad_image = gi0 + gi2 + gfar
    grad_text = gt0 + gt1 + gu0 + gu1
    return sums[0, 0], grad_image, grad_text, sums[0, 1], sums[0, 2]


def solution(mesh):
    fine = Mesh(mesh.devices.reshape(SHAPE), NAMES)
    rows = P(NAMES, None)
    return jax.shard_map(
        local,
        mesh=fine,
        in_specs=(rows, rows, P(NAMES), P(), P()),
        out_specs=(P(), rows, rows, P(), P()),
        check_vma=False,
    )
```

```python
import functools

import jax
import jax.numpy as jnp
from jax import lax
from jax.experimental import pallas as pl
from jax.experimental.pallas import tpu as pltpu
from jax.sharding import Mesh
from jax.sharding import PartitionSpec as P

STEPS = 7
LINES, DEEP = 16, 16
SHAPE = (2, 4, 2, 4, 4, 2, 2)
NAMES = ("y_hi", "y_lo", "x_hi", "z_hi", "z_lo", "core", "x_lo")
F32, BF16 = jnp.float32, jnp.bfloat16
VMEM = pl.BlockSpec(memory_space=pltpu.VMEM)
SMEM = pl.BlockSpec(memory_space=pltpu.SMEM)


def up(b):
    plane, pos = divmod(b, 4)
    if plane % DEEP < DEEP - 1:
        return b + 4
    return (plane + 1) % (LINES * DEEP) * 4 + (pos ^ 1)


def down(b):
    plane, pos = divmod(b, 4)
    if plane % DEEP > 0:
        return b - 4
    return (plane - 1) % (LINES * DEEP) * 4 + (pos ^ 1)


def halves(x):
    high = x.astype(BF16)
    return high, (x - high.astype(F32)).astype(BF16)


def joined(*pairs):
    return tuple(jnp.concatenate(parts, 0) for parts in zip(*pairs))


def product(a, b, dims):
    dot = functools.partial(lax.dot_general, dimension_numbers=(dims, ((), ())), preferred_element_type=F32)
    return dot(a[0], b[0]) + (dot(a[0], b[1]) + dot(a[1], b[0]))


def long_product(a, b, dims):
    left = jnp.concatenate([a[0], a[0], a[1]], dims[0][0])
    right = jnp.concatenate([b[0], b[1], b[0]], dims[1][0])
    return lax.dot_general(left, right, (dims, ((), ())), preferred_element_type=F32)


def gradient(weights, cols, log_scale, product):
    grads = product(halves(weights), cols, ((1,), (0,)))
    return jnp.exp(jnp.full((1, grads.shape[1]), log_scale, F32)) * grads


def tag(packet):
    return packet[128:129, 0:128]


def column(row):
    return jnp.transpose(jnp.broadcast_to(row, (row.shape[1], row.shape[1])))


def weigh(sim, dists, row_ids, col_ids, log_scale, bias, tokens):
    size = 128
    scale = jnp.exp(jnp.full((1, size), log_scale, F32))
    norm = 1.0 / (STEPS * size)
    loss = slope = plain = jnp.zeros((size, size), F32)
    weights = []
    for a, row in enumerate(dists):
        line = []
        mine = column(row_ids[a]) if a < len(row_ids) else None
        for b, (dist, counts) in enumerate(row):
            part = sim[a * size : (a + 1) * size, b * size : (b + 1) * size]
            keep = jnp.where((dist >= 0) & (dist < STEPS) & counts, norm, 0.0).astype(F32)
            if mine is None:
                sign = -1.0
            else:
                other = jnp.where((dist == 0) | (dist == 1), col_ids[b], -1.0)
                sign = jnp.where(mine == other, 1.0, -1.0)
            u = sign * (scale * part + bias)
            small = jnp.exp(-jnp.abs(u))
            weight = -sign * (jnp.where(u >= 0, small, 1.0) / (1.0 + small)) * keep
            loss = loss + (jnp.maximum(-u, 0.0) + jnp.log1p(small)) * keep
            slope = slope + weight * part
            plain = plain + weight
            line.append(weight)
        weights.append(jnp.concatenate(line, 1))
    lane = lax.broadcasted_iota(jnp.int32, (1, size), 1)
    loss, slope, plain = jnp.sum(loss), jnp.sum(scale * slope), jnp.sum(plain)
    sums = jnp.where(lane == 0, loss, jnp.where(lane == 1, slope, jnp.where(lane == 2, plain, 0.0)))
    return jnp.concatenate(weights, 0), sums * (1.0 / tokens)


def pack_kernel(ids, image, text, image_packet, text_packet, arrived):
    size = ids.shape[1]
    packets = (text_packet, image_packet)
    copies = [
        pltpu.make_async_copy(source, packet.at[0:size], arrived.at[n])
        for n, (source, packet) in enumerate(zip((text, image), packets))
    ]
    for copy in copies:
        copy.start()
    for packet in packets:
        packet[size:, :] = jnp.zeros_like(packet[size:, :])
        packet[size : size + 1, 0:size] = ids[...].astype(F32)
    for copy in copies:
        copy.wait()


def first_kernel(
    tokens, place, params, i2, far, t1, u0, image, text, ids,
    high, low, images, gt0, gt1, gu0, tags, sums, i0, t0, held_ids, arrived,
):
    copies = [
        pltpu.make_async_copy(source, target, arrived.at[n])
        for n, (source, target) in enumerate(((image, i0), (text, t0), (ids, held_ids)))
    ]
    for copy in copies:
        copy.start()
    p, q, r, core = place[0], place[1], place[2], place[3]
    size = image.shape[0]
    both = 2 * size
    lone_rows, lone_cols = halves(far[...]), halves(u0[0:size, :])
    sim = product(lone_rows, lone_cols, ((1,), (1,)))
    lone, parts = weigh(sim, [[((r ^ 2) + 8 - q, core == 1)]], (), (), params[0], params[1], tokens)
    images[both:, :] = gradient(lone, lone_cols, params[0], product)
    gu0[...] = gradient(jnp.transpose(lone), lone_rows, params[0], product)
    high[both:, :], low[both:, :] = lone_rows
    mate_rows, near_cols = halves(i2[0:size, :]), halves(t1[0:size, :])
    for copy in copies:
        copy.wait()
    rows = joined(halves(i0[...]), mate_rows)
    high[0:both, :], low[0:both, :] = rows
    cols = joined(halves(t0[...]), near_cols, lone_cols)
    dists = [[(i - p, True), (i - (p ^ 1), True), (i + 4 - q, True)] for i in (p, p ^ 2)]
    sim = long_product(rows, cols, ((1,), (1,)))
    own, mate = held_ids[...].astype(F32), tag(i2)
    tags[0:1, :], tags[1:2, :] = own, mate
    row_ids, col_ids = (own, mate), (own, tag(t1), tag(u0))
    weights, more = weigh(sim, dists, row_ids, col_ids, params[0], params[1], tokens)
    sums[...] = parts + more
    images[0:both, :] = gradient(weights, cols, params[0], long_product)
    texts = gradient(jnp.transpose(weights), rows, params[0], long_product)
    gt0[...] = texts[0:size, :]
    gt1[...] = texts[size:both, :]
    gu0[...] += texts[both:, :]


def last_kernel(tokens, place, params, tags, high, low, u1, images, sums_in, gi0, gi2, gfar, gu1, sums):
    p, q, r, core = place[0], place[1], place[2], place[3]
    size = tags.shape[1]
    rows, cols = (high[...], low[...]), halves(u1[0:size, :])
    dists = [[(i + 4 - (q ^ 1), True)] for i in (p, p ^ 2)]
    dists.append([((r ^ 2) + 8 - (q ^ 1), core == 1)])
    sim = product(rows, cols, ((1,), (1,)))
    weights, parts = weigh(sim, dists, (tags[0:1, :], tags[1:2, :]), (tag(u1),), params[0], params[1], tokens)
    sums[...] = sums_in[...] + parts
    grads = images[...] + gradient(weights, cols, params[0], product)
    gi0[...] = grads[0:size, :]
    gi2[...] = grads[size : 2 * size, :]
    gfar[...] = grads[2 * size :, :]
    gu1[...] = gradient(jnp.transpose(weights), rows, params[0], product)


def pack(ids, image, text):
    plain = pl.BlockSpec(memory_space=pltpu.HBM)
    size, width = image.shape
    packet = jax.ShapeDtypeStruct((size + 8, width), F32)
    image, text = (pltpu.with_memory_space_constraint(x, pltpu.HBM) for x in (image, text))
    return pl.pallas_call(
        pack_kernel,
        out_shape=[packet] * 2,
        in_specs=[VMEM, plain, plain],
        out_specs=[VMEM] * 2,
        scratch_shapes=[pltpu.SemaphoreType.DMA((2,))],
        cost_estimate=pl.CostEstimate(flops=0, bytes_accessed=2 << 21, transcendentals=0),
        name="pack",
    )(ids, image, text)


def kernel_call(body, name, shapes, rows, cols, *args, plain=0):
    cost = pl.CostEstimate(
        flops=18 * rows * cols * 1152, bytes_accessed=8 * 1152 * (rows + cols), transcendentals=2 * rows * cols
    )
    near = len(args) - plain
    far = [pltpu.with_memory_space_constraint(arg, pltpu.HBM) for arg in args[near:]]
    return pl.pallas_call(
        body,
        out_shape=[jax.ShapeDtypeStruct(shape, dtype) for shape, dtype in shapes],
        in_specs=[SMEM, SMEM] + [VMEM] * (near - 2) + [pl.BlockSpec(memory_space=pltpu.HBM)] * plain,
        out_specs=[VMEM] * len(shapes),
        scratch_shapes=[pltpu.VMEM(arg.shape, arg.dtype) for arg in far]
        + [pltpu.SemaphoreType.DMA((plain,))] * (plain > 0),
        compiler_params=pltpu.CompilerParams(vmem_limit_bytes=16 << 20),
        cost_estimate=cost,
        name=name,
    )(*args[:near], *far)


def local(image, text, video_ids, log_scale, bias):
    size, width = image.shape
    count = lax.axis_size(NAMES)
    tokens = size * count
    everyone = range(count)

    def send(x, to, senders=everyone):
        return lax.ppermute(x, NAMES, [(b, to(b)) for b in senders])

    def other_core(x):
        return send(x, lambda b: b ^ 2)

    def beside(x):
        return send(x, lambda b: b ^ 1)

    plane_z = lax.axis_index(("z_hi", "z_lo"))
    core = lax.axis_index("core")
    p = 2 * core + lax.axis_index("x_lo")
    q = jnp.where(plane_z > 0, p, p ^ 1)
    r = jnp.where(plane_z < DEEP - 1, p, p ^ 1)
    place = jnp.stack([p, q, r, core]).astype(jnp.int32)
    params = jnp.stack([log_scale, bias])

    own = video_ids[None]
    image_packet, text_packet = pack(own, image, text)
    t1 = beside(text_packet)
    u0 = send(text_packet, up)
    far = send(image, lambda b: down(b) ^ 2, [b for b in everyone if b % 4 < 2])
    i2 = other_core(image_packet)
    t1, far, place, params = lax.optimization_barrier((t1, far, place, params))
    u1 = send(t1, up)

    block, three, row = ((size, width), F32), (3 * size, width), ((1, size), F32)
    high, low, images, gt0, gt1, gu0, tags, sums = kernel_call(
        functools.partial(first_kernel, tokens),
        "first",
        [(three, BF16), (three, BF16), (three, F32), block, block, block, ((2, size), F32), row],
        384,
        384,
        *(place, params, i2, far, t1, u0, image, text, own),
        plain=3,
    )
    gt1, gu0 = beside(gt1), send(gu0, down)
    gi0, gi2, gfar, gu1, sums = kernel_call(
        functools.partial(last_kernel, tokens),
        "last",
        [block, block, block, block, row],
        384,
        128,
        *(place, params, tags, high, low, u1, images, sums),
    )
    gu1 = send(gu1, lambda b: down(b) ^ 1)
    gi2 = other_core(gi2)
    gfar = send(gfar, lambda b: up(b) ^ 2, [b for b in everyone if b % 4 >= 2])

    def add_up(row, axes):
        shares = jnp.broadcast_to(row, (lax.axis_size(axes), size))
        return jnp.sum(lax.all_to_all(shares, axes, 0, 0, tiled=True), axis=0, keepdims=True)

    sums = add_up(sums, ("y_hi", "y_lo", "x_hi", "core", "x_lo"))
    sums, gt1, gu0, gu1, gi2, gfar = lax.optimization_barrier((sums, gt1, gu0, gu1, gi2, gfar))
    sums = add_up(sums, ("z_hi", "z_lo"))
    grad_image = gi0 + gi2 + gfar
    grad_text = gt0 + gt1 + gu0 + gu1
    return sums[0, 0], grad_image, grad_text, sums[0, 1], sums[0, 2]


def solution(mesh):
    fine = Mesh(mesh.devices.reshape(SHAPE), NAMES)
    rows = P(NAMES, None)
    return jax.shard_map(
        local,
        mesh=fine,
        in_specs=(rows, rows, P(NAMES), P(), P()),
        out_specs=(P(), rows, rows, P(), P()),
        check_vma=False,
    )
```

```python
import functools

import jax
import jax.numpy as jnp
from jax import lax
from jax.experimental import pallas as pl
from jax.experimental.pallas import tpu as pltpu
from jax.sharding import Mesh
from jax.sharding import PartitionSpec as P

STEPS = 7
LINES, DEEP = 16, 16
SHAPE = (2, 4, 2, 4, 4, 2, 2)
NAMES = ("y_hi", "y_lo", "x_hi", "z_hi", "z_lo", "core", "x_lo")
F32, BF16 = jnp.float32, jnp.bfloat16
VMEM = pl.BlockSpec(memory_space=pltpu.VMEM)
SMEM = pl.BlockSpec(memory_space=pltpu.SMEM)


def up(b):
    plane, pos = divmod(b, 4)
    if plane % DEEP < DEEP - 1:
        return b + 4
    return (plane + 1) % (LINES * DEEP) * 4 + (pos ^ 1)


def down(b):
    plane, pos = divmod(b, 4)
    if plane % DEEP > 0:
        return b - 4
    return (plane - 1) % (LINES * DEEP) * 4 + (pos ^ 1)


def halves(x):
    high = x.astype(BF16)
    return high, (x - high.astype(F32)).astype(BF16)


def joined(*pairs):
    return tuple(jnp.concatenate(parts, 0) for parts in zip(*pairs))


def product(a, b, dims):
    dot = functools.partial(lax.dot_general, dimension_numbers=(dims, ((), ())), preferred_element_type=F32)
    return dot(a[0], b[0]) + (dot(a[0], b[1]) + dot(a[1], b[0]))


def long_product(a, b, dims):
    left = jnp.concatenate([a[0], a[0], a[1]], dims[0][0])
    right = jnp.concatenate([b[0], b[1], b[0]], dims[1][0])
    return lax.dot_general(left, right, (dims, ((), ())), preferred_element_type=F32)


def gradient(weights, cols, log_scale, product):
    grads = product(halves(weights), cols, ((1,), (0,)))
    return jnp.exp(jnp.full((1, grads.shape[1]), log_scale, F32)) * grads


def tag(packet):
    return packet[128:129, 0:128]


def column(row):
    return jnp.transpose(jnp.broadcast_to(row, (row.shape[1], row.shape[1])))


def weigh(sim, dists, row_ids, col_ids, log_scale, bias, tokens):
    size = 128
    scale = jnp.exp(jnp.full((1, size), log_scale, F32))
    norm = 1.0 / (STEPS * size)
    loss = slope = plain = jnp.zeros((size, size), F32)
    weights = []
    for a, row in enumerate(dists):
        line = []
        mine = column(row_ids[a]) if a < len(row_ids) else None
        for b, (dist, counts) in enumerate(row):
            part = sim[a * size : (a + 1) * size, b * size : (b + 1) * size]
            keep = jnp.where((dist >= 0) & (dist < STEPS) & counts, norm, 0.0).astype(F32)
            if mine is None:
                sign = -1.0
            else:
                other = jnp.where((dist == 0) | (dist == 1), col_ids[b], -1.0)
                sign = jnp.where(mine == other, 1.0, -1.0)
            u = sign * (scale * part + bias)
            small = jnp.exp(-jnp.abs(u))
            weight = -sign * (jnp.where(u >= 0, small, 1.0) / (1.0 + small)) * keep
            loss = loss + (jnp.maximum(-u, 0.0) + jnp.log1p(small)) * keep
            slope = slope + weight * part
            plain = plain + weight
            line.append(weight)
        weights.append(jnp.concatenate(line, 1))
    lane = lax.broadcasted_iota(jnp.int32, (1, size), 1)
    loss, slope, plain = jnp.sum(loss), jnp.sum(scale * slope), jnp.sum(plain)
    sums = jnp.where(lane == 0, loss, jnp.where(lane == 1, slope, jnp.where(lane == 2, plain, 0.0)))
    return jnp.concatenate(weights, 0), sums * (1.0 / tokens)


def pack_kernel(ids, image, packet, arrived):
    size = image.shape[0]
    copy = pltpu.make_async_copy(image, packet.at[0:size], arrived)
    copy.start()
    packet[size:, :] = jnp.zeros_like(packet[size:, :])
    packet[size : size + 1, 0:size] = ids[...].astype(F32)
    copy.wait()


def first_kernel(
    tokens, place, params, before, i2, far, t1, u0, image, text, ids,
    high, low, images, gt0, gt1, gu0, tags, sums, i0, t0, held_ids, arrived, back, left,
):
    copies = [
        pltpu.make_async_copy(source, target, arrived.at[n])
        for n, (source, target) in enumerate(((image, i0), (text, t0), (ids, held_ids)))
    ]
    for copy in copies:
        copy.start()
    p, q, r, core = place[0], place[1], place[2], place[3]
    size = image.shape[0]
    both = 2 * size
    lone_rows, lone_cols = halves(far[...]), halves(u0[...])
    sim = product(lone_rows, lone_cols, ((1,), (1,)))
    lone, parts = weigh(sim, [[((r ^ 2) + 8 - q, core == 1)]], (), (), params[0], params[1], tokens)
    images[both:, :] = gradient(lone, lone_cols, params[0], long_product)
    lone_texts = gradient(jnp.transpose(lone), lone_rows, params[0], long_product)
    high[both:, :], low[both:, :] = lone_rows
    mate_rows, near_cols = halves(i2[0:size, :]), halves(t1[...])
    for copy in copies:
        copy.wait()
    rows = joined(halves(i0[...]), mate_rows)
    high[0:both, :], low[0:both, :] = rows
    cols = joined(halves(t0[...]), near_cols, lone_cols)
    dists = [[(i - p, True), (i - (p ^ 1), True), (i + 4 - q, True)] for i in (p, p ^ 2)]
    sim = long_product(rows, cols, ((1,), (1,)))
    own, mate, last = held_ids[...].astype(F32), tag(i2), before[...].astype(F32)
    tags[0:1, :], tags[1:2, :], tags[2:3, :] = own, mate, last
    row_ids, col_ids = (own, mate), (own, last, last)
    weights, more = weigh(sim, dists, row_ids, col_ids, params[0], params[1], tokens)
    sums[...] = parts + more
    texts = gradient(jnp.transpose(weights), rows, params[0], long_product)
    back[0:size, :] = texts[size:both, :]
    back[size:, :] = texts[both:, :] + lone_texts
    copies = [
        pltpu.make_async_copy(back.at[n * size : (n + 1) * size], target, left.at[n])
        for n, target in enumerate((gt1, gu0))
    ]
    for copy in copies:
        copy.start()
    gt0[...] = texts[0:size, :]
    images[0:both, :] = gradient(weights, cols, params[0], long_product)
    for copy in copies:
        copy.wait()


def last_kernel(tokens, place, params, tags, high, low, u1, images, sums_in, gi0, gi2, gfar, gu1, sums):
    p, q, r, core = place[0], place[1], place[2], place[3]
    size = tags.shape[1]
    rows, cols = (high[...], low[...]), halves(u1[...])
    dists = [[(i + 4 - (q ^ 1), True)] for i in (p, p ^ 2)]
    dists.append([((r ^ 2) + 8 - (q ^ 1), core == 1)])
    sim = product(rows, cols, ((1,), (1,)))
    weights, parts = weigh(sim, dists, (tags[0:1, :], tags[1:2, :]), (tags[2:3, :],), params[0], params[1], tokens)
    sums[...] = sums_in[...] + parts
    grads = images[...] + gradient(weights, cols, params[0], product)
    gi0[...] = grads[0:size, :]
    gi2[...] = grads[size : 2 * size, :]
    gfar[...] = grads[2 * size :, :]
    gu1[...] = gradient(jnp.transpose(weights), rows, params[0], product)


def pack(ids, image):
    size, width = image.shape
    return pl.pallas_call(
        pack_kernel,
        out_shape=jax.ShapeDtypeStruct((size + 8, width), F32),
        in_specs=[VMEM, pl.BlockSpec(memory_space=pltpu.HBM)],
        out_specs=VMEM,
        scratch_shapes=[pltpu.SemaphoreType.DMA],
        cost_estimate=pl.CostEstimate(flops=0, bytes_accessed=1 << 21, transcendentals=0),
        name="pack",
    )(ids, pltpu.with_memory_space_constraint(image, pltpu.HBM))


def kernel_call(body, name, shapes, rows, cols, *args, plain=0, out=()):
    cost = pl.CostEstimate(
        flops=18 * rows * cols * 1152, bytes_accessed=8 * 1152 * (rows + cols), transcendentals=2 * rows * cols
    )
    near = len(args) - plain
    far = [pltpu.with_memory_space_constraint(arg, pltpu.HBM) for arg in args[near:]]
    return pl.pallas_call(
        body,
        out_shape=[jax.ShapeDtypeStruct(shape, dtype) for shape, dtype in shapes],
        in_specs=[SMEM, SMEM] + [VMEM] * (near - 2) + [pl.BlockSpec(memory_space=pltpu.HBM)] * plain,
        out_specs=[pl.BlockSpec(memory_space=pl.ANY) if n in out else VMEM for n in range(len(shapes))],
        scratch_shapes=[pltpu.VMEM(arg.shape, arg.dtype) for arg in far]
        + [pltpu.SemaphoreType.DMA((plain,))] * (plain > 0)
        + [pltpu.VMEM((256, 1152), F32), pltpu.SemaphoreType.DMA((2,))] * (len(out) > 0),
        compiler_params=pltpu.CompilerParams(vmem_limit_bytes=16 << 20),
        cost_estimate=cost,
        name=name,
    )(*args[:near], *far)


def local(image, text, video_ids, log_scale, bias):
    size, width = image.shape
    count = lax.axis_size(NAMES)
    tokens = size * count
    everyone = range(count)

    def send(x, to, senders=everyone):
        return lax.ppermute(x, NAMES, [(b, to(b)) for b in senders])

    def other_core(x):
        return send(x, lambda b: b ^ 2)

    def beside(x):
        return send(x, lambda b: b ^ 1)

    plane_z = lax.axis_index(("z_hi", "z_lo"))
    core = lax.axis_index("core")
    p = 2 * core + lax.axis_index("x_lo")
    q = jnp.where(plane_z > 0, p, p ^ 1)
    r = jnp.where(plane_z < DEEP - 1, p, p ^ 1)
    place = jnp.stack([p, q, r, core]).astype(jnp.int32)
    params = jnp.stack([log_scale, bias])

    own = video_ids[None]
    t1 = beside(text)
    u0 = send(text, up)
    far = send(image, lambda b: down(b) ^ 2, [b for b in everyone if b % 4 < 2])
    before = send(own, lambda b: (b ^ 1) if b % 4 < 3 else (b + 3) % count)
    i2 = other_core(pack(own, image))
    t1, u0, far, before, place, params = lax.optimization_barrier((t1, u0, far, before, place, params))
    u1 = send(t1, up)

    block, three, row = ((size, width), F32), (3 * size, width), ((1, size), F32)
    high, low, images, gt0, gt1, gu0, tags, sums = kernel_call(
        functools.partial(first_kernel, tokens),
        "first",
        [(three, BF16), (three, BF16), (three, F32), block, block, block, ((3, size), F32), row],
        384,
        384,
        *(place, params, before, i2, far, t1, u0, image, text, own),
        plain=3,
        out=(4, 5),
    )
    gt1, gu0 = beside(gt1), send(gu0, down)
    gi0, gi2, gfar, gu1, sums = kernel_call(
        functools.partial(last_kernel, tokens),
        "last",
        [block, block, block, block, row],
        384,
        128,
        *(place, params, tags, high, low, u1, images, sums),
    )
    gu1 = send(gu1, lambda b: down(b) ^ 1)
    gi2 = other_core(gi2)
    gfar = send(gfar, lambda b: up(b) ^ 2, [b for b in everyone if b % 4 >= 2])

    def add_up(row, axes):
        shares = jnp.broadcast_to(row, (lax.axis_size(axes), size))
        return jnp.sum(lax.all_to_all(shares, axes, 0, 0, tiled=True), axis=0, keepdims=True)

    sums = add_up(sums, ("y_hi", "y_lo", "x_hi", "core", "x_lo"))
    sums, gt1, gu0, gu1, gi2, gfar = lax.optimization_barrier((sums, gt1, gu0, gu1, gi2, gfar))
    sums = add_up(sums, ("z_hi", "z_lo"))
    grad_image = gi0 + gi2 + gfar
    grad_text = gt0 + gt1 + gu0 + gu1
    return sums[0, 0], grad_image, grad_text, sums[0, 1], sums[0, 2]


def solution(mesh):
    fine = Mesh(mesh.devices.reshape(SHAPE), NAMES)
    rows = P(NAMES, None)
    return jax.shard_map(
        local,
        mesh=fine,
        in_specs=(rows, rows, P(NAMES), P(), P()),
        out_specs=(P(), rows, rows, P(), P()),
        check_vma=False,
    )
```

```python
import functools

import jax
import jax.numpy as jnp
from jax import lax
from jax.experimental import pallas as pl
from jax.experimental.pallas import tpu as pltpu
from jax.sharding import Mesh
from jax.sharding import PartitionSpec as P

STEPS = 7
LINES, DEEP = 16, 16
SHAPE = (2, 4, 2, 4, 4, 2, 2)
NAMES = ("y_hi", "y_lo", "x_hi", "z_hi", "z_lo", "core", "x_lo")
F32, BF16 = jnp.float32, jnp.bfloat16
VMEM = pl.BlockSpec(memory_space=pltpu.VMEM)
SMEM = pl.BlockSpec(memory_space=pltpu.SMEM)


def up(b):
    plane, pos = divmod(b, 4)
    if plane % DEEP < DEEP - 1:
        return b + 4
    return (plane + 1) % (LINES * DEEP) * 4 + (pos ^ 1)


def down(b):
    plane, pos = divmod(b, 4)
    if plane % DEEP > 0:
        return b - 4
    return (plane - 1) % (LINES * DEEP) * 4 + (pos ^ 1)


def halves(x):
    high = x.astype(BF16)
    return high, (x - high.astype(F32)).astype(BF16)


def joined(*pairs):
    return tuple(jnp.concatenate(parts, 0) for parts in zip(*pairs))


def product(a, b, dims):
    dot = functools.partial(lax.dot_general, dimension_numbers=(dims, ((), ())), preferred_element_type=F32)
    return dot(a[0], b[0]) + (dot(a[0], b[1]) + dot(a[1], b[0]))


def long_product(a, b, dims):
    left = jnp.concatenate([a[0], a[0], a[1]], dims[0][0])
    right = jnp.concatenate([b[0], b[1], b[0]], dims[1][0])
    return lax.dot_general(left, right, (dims, ((), ())), preferred_element_type=F32)


def gradient(weights, cols, log_scale, product):
    grads = product(halves(weights), cols, ((1,), (0,)))
    return jnp.exp(jnp.full((1, grads.shape[1]), log_scale, F32)) * grads


def tag(packet):
    return packet[128:129, 0:128]


def column(row):
    return jnp.transpose(jnp.broadcast_to(row, (row.shape[1], row.shape[1])))


def weigh(sim, dists, row_ids, col_ids, log_scale, bias, tokens):
    size = 128
    scale = jnp.exp(jnp.full((1, size), log_scale, F32))
    norm = 1.0 / (STEPS * size)
    loss = slope = plain = jnp.zeros((size, size), F32)
    weights = []
    for a, row in enumerate(dists):
        line = []
        mine = column(row_ids[a]) if a < len(row_ids) else None
        for b, (dist, counts) in enumerate(row):
            part = sim[a * size : (a + 1) * size, b * size : (b + 1) * size]
            keep = jnp.where((dist >= 0) & (dist < STEPS) & counts, norm, 0.0).astype(F32)
            if mine is None:
                sign = -1.0
            else:
                other = jnp.where((dist == 0) | (dist == 1), col_ids[b], -1.0)
                sign = jnp.where(mine == other, 1.0, -1.0)
            u = sign * (scale * part + bias)
            small = jnp.exp(-jnp.abs(u))
            weight = -sign * (jnp.where(u >= 0, small, 1.0) / (1.0 + small)) * keep
            loss = loss + (jnp.maximum(-u, 0.0) + jnp.log1p(small)) * keep
            slope = slope + weight * part
            plain = plain + weight
            line.append(weight)
        weights.append(jnp.concatenate(line, 1))
    lane = lax.broadcasted_iota(jnp.int32, (1, size), 1)
    loss, slope, plain = jnp.sum(loss), jnp.sum(scale * slope), jnp.sum(plain)
    sums = jnp.where(lane == 0, loss, jnp.where(lane == 1, slope, jnp.where(lane == 2, plain, 0.0)))
    return jnp.concatenate(weights, 0), sums * (1.0 / tokens)


def pack_kernel(ids, image, packet, arrived):
    size = image.shape[0]
    copy = pltpu.make_async_copy(image, packet.at[0:size], arrived)
    copy.start()
    packet[size:, :] = jnp.zeros_like(packet[size:, :])
    packet[size : size + 1, 0:size] = ids[...].astype(F32)
    copy.wait()


def first_kernel(
    tokens, place, params, before, i2, far, t1, u0, image, text, ids,
    high, low, images, gt0, gt1, gu0, tags, sums, i0, t0, held_ids, arrived, back, left,
):
    copies = [
        pltpu.make_async_copy(source, target, arrived.at[n])
        for n, (source, target) in enumerate(((image, i0), (text, t0), (ids, held_ids)))
    ]
    for copy in copies:
        copy.start()
    p, q, r, core = place[0], place[1], place[2], place[3]
    size = image.shape[0]
    both = 2 * size
    lone_rows, lone_cols = halves(far[...]), halves(u0[...])
    sim = product(lone_rows, lone_cols, ((1,), (1,)))
    lone, parts = weigh(sim, [[((r ^ 2) + 8 - q, core == 1)]], (), (), params[0], params[1], tokens)
    images[both:, :] = gradient(lone, lone_cols, params[0], long_product)
    lone_texts = gradient(jnp.transpose(lone), lone_rows, params[0], long_product)
    high[both:, :], low[both:, :] = lone_rows
    mate_rows, near_cols = halves(i2[0:size, :]), halves(t1[...])
    for copy in copies:
        copy.wait()
    rows = joined(halves(i0[...]), mate_rows)
    high[0:both, :], low[0:both, :] = rows
    cols = joined(halves(t0[...]), near_cols, lone_cols)
    dists = [[(i - p, True), (i - (p ^ 1), True), (i + 4 - q, True)] for i in (p, p ^ 2)]
    sim = long_product(rows, cols, ((1,), (1,)))
    own, mate, last = held_ids[...].astype(F32), tag(i2), before[...].astype(F32)
    tags[0:1, :], tags[1:2, :], tags[2:3, :] = own, mate, last
    row_ids, col_ids = (own, mate), (own, last, last)
    weights, more = weigh(sim, dists, row_ids, col_ids, params[0], params[1], tokens)
    sums[...] = parts + more
    texts = gradient(jnp.transpose(weights), rows, params[0], long_product)
    back[0:size, :] = texts[size:both, :]
    back[size:, :] = texts[both:, :] + lone_texts
    copies = [
        pltpu.make_async_copy(back.at[n * size : (n + 1) * size], target, left.at[n])
        for n, target in enumerate((gt1, gu0))
    ]
    for copy in copies:
        copy.start()
    gt0[...] = texts[0:size, :]
    images[0:both, :] = gradient(weights, cols, params[0], long_product)
    for copy in copies:
        copy.wait()


def last_kernel(tokens, place, params, tags, high, low, u1, images, sums_in, gi0, gi2, gfar, gu1, sums):
    p, q, r, core = place[0], place[1], place[2], place[3]
    size = tags.shape[1]
    rows, cols = (high[...], low[...]), halves(u1[...])
    dists = [[(i + 4 - (q ^ 1), True)] for i in (p, p ^ 2)]
    dists.append([((r ^ 2) + 8 - (q ^ 1), core == 1)])
    sim = product(rows, cols, ((1,), (1,)))
    weights, parts = weigh(sim, dists, (tags[0:1, :], tags[1:2, :]), (tags[2:3, :],), params[0], params[1], tokens)
    sums[...] = sums_in[...] + parts
    grads = images[...] + gradient(weights, cols, params[0], product)
    gi0[...] = grads[0:size, :]
    gi2[...] = grads[size : 2 * size, :]
    gfar[...] = grads[2 * size :, :]
    gu1[...] = gradient(jnp.transpose(weights), rows, params[0], product)


def pack(ids, image):
    size, width = image.shape
    return pl.pallas_call(
        pack_kernel,
        out_shape=jax.ShapeDtypeStruct((size + 8, width), F32),
        in_specs=[VMEM, pl.BlockSpec(memory_space=pltpu.HBM)],
        out_specs=VMEM,
        scratch_shapes=[pltpu.SemaphoreType.DMA],
        cost_estimate=pl.CostEstimate(flops=0, bytes_accessed=1 << 21, transcendentals=0),
        name="pack",
    )(ids, pltpu.with_memory_space_constraint(image, pltpu.HBM))


def kernel_call(body, name, shapes, rows, cols, *args, plain=0, out=()):
    cost = pl.CostEstimate(
        flops=18 * rows * cols * 1152, bytes_accessed=8 * 1152 * (rows + cols), transcendentals=2 * rows * cols
    )
    near = len(args) - plain
    far = [pltpu.with_memory_space_constraint(arg, pltpu.HBM) for arg in args[near:]]
    return pl.pallas_call(
        body,
        out_shape=[jax.ShapeDtypeStruct(shape, dtype) for shape, dtype in shapes],
        in_specs=[SMEM, SMEM] + [VMEM] * (near - 2) + [pl.BlockSpec(memory_space=pltpu.HBM)] * plain,
        out_specs=[pl.BlockSpec(memory_space=pl.ANY) if n in out else VMEM for n in range(len(shapes))],
        scratch_shapes=[pltpu.VMEM(arg.shape, arg.dtype) for arg in far]
        + [pltpu.SemaphoreType.DMA((plain,))] * (plain > 0)
        + [pltpu.VMEM((256, 1152), F32), pltpu.SemaphoreType.DMA((2,))] * (len(out) > 0),
        compiler_params=pltpu.CompilerParams(vmem_limit_bytes=16 << 20),
        cost_estimate=cost,
        name=name,
    )(*args[:near], *far)


def local(image, text, video_ids, log_scale, bias):
    size, width = image.shape
    count = lax.axis_size(NAMES)
    tokens = size * count
    everyone = range(count)

    def send(x, to, senders=everyone):
        return lax.ppermute(x, NAMES, [(b, to(b)) for b in senders])

    def other_core(x):
        return send(x, lambda b: b ^ 2)

    def beside(x):
        return send(x, lambda b: b ^ 1)

    plane_z = lax.axis_index(("z_hi", "z_lo"))
    core = lax.axis_index("core")
    p = 2 * core + lax.axis_index("x_lo")
    q = jnp.where(plane_z > 0, p, p ^ 1)
    r = jnp.where(plane_z < DEEP - 1, p, p ^ 1)
    place = jnp.stack([p, q, r, core]).astype(jnp.int32)
    params = jnp.stack([log_scale, bias])

    own = video_ids[None]
    t1 = beside(text)
    u0 = send(text, up)
    far = send(image, lambda b: down(b) ^ 2, [b for b in everyone if b % 4 < 2])
    before = send(own, lambda b: (b ^ 1) if b % 4 < 3 else (b + 3) % count)
    i2 = other_core(pack(own, image))
    t1, u0, far, before, place, params = lax.optimization_barrier((t1, u0, far, before, place, params))
    u1 = send(t1, up)

    block, three, row = ((size, width), F32), (3 * size, width), ((1, size), F32)
    high, low, images, gt0, gt1, gu0, tags, sums = kernel_call(
        functools.partial(first_kernel, tokens),
        "first",
        [(three, BF16), (three, BF16), (three, F32), block, block, block, ((3, size), F32), row],
        384,
        384,
        *(place, params, before, i2, far, t1, u0, image, text, own),
        plain=3,
        out=(4, 5),
    )
    gt1, gu0 = beside(gt1), send(gu0, down)
    gi0, gi2, gfar, gu1, sums = kernel_call(
        functools.partial(last_kernel, tokens),
        "last",
        [block, block, block, block, row],
        384,
        128,
        *(place, params, tags, high, low, u1, images, sums),
    )
    gu1 = send(gu1, lambda b: down(b) ^ 1)
    gi2 = other_core(gi2)
    gt1, gu0, gi2, gfar = lax.optimization_barrier((gt1, gu0, gi2, gfar))
    gfar = send(gfar, lambda b: up(b) ^ 2, [b for b in everyone if b % 4 >= 2])

    def add_up(row, axes):
        shares = jnp.broadcast_to(row, (lax.axis_size(axes), size))
        return jnp.sum(lax.all_to_all(shares, axes, 0, 0, tiled=True), axis=0, keepdims=True)

    sums = add_up(sums, ("y_hi", "y_lo", "x_hi", "core", "x_lo"))
    sums, gt1, gu0, gu1, gi2, gfar = lax.optimization_barrier((sums, gt1, gu0, gu1, gi2, gfar))
    sums = add_up(sums, ("z_hi", "z_lo"))
    grad_image = gi0 + gi2 + gfar
    grad_text = gt0 + gt1 + gu0 + gu1
    return sums[0, 0], grad_image, grad_text, sums[0, 1], sums[0, 2]


def solution(mesh):
    fine = Mesh(mesh.devices.reshape(SHAPE), NAMES)
    rows = P(NAMES, None)
    return jax.shard_map(
        local,
        mesh=fine,
        in_specs=(rows, rows, P(NAMES), P(), P()),
        out_specs=(P(), rows, rows, P(), P()),
        check_vma=False,
    )
```
